32 devices in a mesh: rep: 2 (over y), tp: 8 (over z, x), sub: 2 (over core).
Axes of the slice: x: 2, y: 2, z: 4, core: 2. Of those that a mesh axis runs over, the one named last changes fastest.
Arguments:
- query: bfloat16 [64, 8, 128], P(('rep', 'sub'), 'tp'), parts along dimension 0, may hold values from -6 to 6
- new_key: bfloat16 [64, 8, 128], P(('rep', 'sub'), 'tp'), parts along dimension 0, may hold values from -5 to 5
- new_value: bfloat16 [64, 8, 128], P(('rep', 'sub'), 'tp'), parts along dimension 0, may hold values from -12 to 12
- cache_keys: bfloat16 [8, 64, 192, 128], P('tp', ('rep', 'sub')), parts along dimension 1, may hold values from -6 to 6, as said below
- cache_values: bfloat16 [8, 64, 192, 128], P('tp', ('rep', 'sub')), parts along dimension 1, may hold values from -12 to 12, as said below
- lengths: int32 [64], P(('rep', 'sub')), parts along dimension 0, may hold values from 2 to 192, as said below
- out_weight: bfloat16 [1024, 16384], P(('tp', 'sub')), may hold values from -0.25 to 0.25
- residual: bfloat16 [64, 16384], P('rep', ('tp', 'sub')), parts along dimension 0, may hold values from -6 to 6
Outputs:
- stream: bfloat16 [64, 16384], P('rep'), parts along dimension 0
The draws below stay inside these ranges and needn't reach their ends.
There are 2 independent parts, one for each index of `rep`. The reference program is written for one: setup_inputs(seed, part) draws one part's arguments, and reference() takes and returns one part's arrays. A program takes and returns all parts, laid end to end along the dimension named above; an argument that names none is the same for every part. Nothing has to cross between parts.
Inputs may be any that keep to these rules, and one draw needn't show every extreme that they name: `lengths`: each row's count of filled slots; some row in every draw fills all 192 slots. cache_keys[h] equals cache_keys[h2] whenever h // 8 == h2 // 8. cache_values[h] equals cache_values[h2] whenever h // 8 == h2 // 8.
All inputs are finite; a program needn't handle non-finite values.
Results may differ from the reference program's by a relative error of at most 0.0049.
Values may be sent and summed in bfloat16 or wider, within the bound.
A program may use at most 64 MiB of HBM per device.

```python
import math
import jax
import jax.numpy as jnp
from jax import lax

D = 16384
HD = 128
HEAD_DEV = 1
HEADS = 8
KV_HEADS = 1
GROUP = 8
ROWS = 32
CTX = 192
N_SUB = 2


def draw_query(key, part):
    key = jax.random.fold_in(key, 11)
    values = jnp.clip(jax.random.normal(key, (ROWS, HEADS, HD), jnp.float32), -4.0, 4.0)
    return values.astype(jnp.bfloat16)


def draw_cache_keys(key, part):
    key = jax.random.fold_in(key, 13)
    values = jnp.clip(jax.random.normal(key, (KV_HEADS, ROWS, CTX, HD), jnp.float32), -4.0, 4.0)
    return jnp.repeat(values, GROUP, axis=0).astype(jnp.bfloat16)


def draw_cache_values(key, part):
    key = jax.random.fold_in(key, 17)
    values = jnp.clip(3.0 * jax.random.normal(key, (KV_HEADS, ROWS, CTX, HD), jnp.float32), -12.0, 12.0)
    return jnp.repeat(values, GROUP, axis=0).astype(jnp.bfloat16)


def draw_lengths(key, part):
    key = jax.random.fold_in(key, 5)
    key_len, key_pick = jax.random.split(key)
    filled = jax.random.randint(key_len, (ROWS,), 2, CTX + 1, dtype=jnp.int32)
    pick = jax.random.randint(key_pick, (), 0, ROWS, dtype=jnp.int32)
    return jnp.where(jnp.arange(ROWS, dtype=jnp.int32) == pick, CTX, filled).astype(jnp.int32)


def strengthened(result, own_key, source, target, blocks, factor):
    owner, partner = [(jnp.arange(result.shape[axis_at]) // (result.shape[axis_at] // blocks)).reshape([-1 if axis == axis_at else 1 for axis in range(result.ndim)]) for axis_at in (source, target)]
    chosen = jax.random.permutation(own_key, blocks)[partner]
    strong = (owner == chosen) | (owner == (partner + blocks // 2) % blocks)
    return jnp.where(strong, factor * result, result)


def block_scale(stream_key, dims, pieces, low, top_value):
    level, own = 1.0, jax.random.fold_in(stream_key, 6)
    for dim, shards_of in pieces:
        draws = jnp.exp(jax.random.uniform(jax.random.fold_in(own, dim), (shards_of,), jnp.float32, low / len(pieces), top_value / len(pieces)))
        level = level * jnp.repeat(draws, dims[dim] // shards_of).reshape([-1 if axis == dim else 1 for axis in range(len(dims))])
    return level


def scatter_about(rng, extent, scale, most, shards=(), held_as=jnp.bfloat16):
    values = jax.random.normal(rng, extent, jnp.float32) * scale
    if len(shards) > 0:
        values = block_scale(rng, extent, shards, -0.22, 0.18) * values
    return jnp.clip(values, min=-most, max=most).astype(held_as)


def bell_draw_with(rng, shape, spread, bound, pieces, heavy, kind=jnp.bfloat16):
    values = spread * jax.random.normal(rng, shape, jnp.float32)
    if pieces:
        values = values * block_scale(rng, shape, pieces, -0.22, 0.18)
    return jnp.clip(strengthened(values, jax.random.fold_in(rng, 3), *heavy), -bound, bound).astype(kind)


def setup_inputs(seed: int = 0, part: int = 0) -> dict:
    arg_keys = jax.random.split(jax.random.key(seed), 9)
    part_keys = jax.random.split(jax.random.fold_in(arg_keys[8], part), 9)
    query = draw_query(jax.random.fold_in(jax.random.fold_in(arg_keys[8], part), 71), part)
    new_key = scatter_about(part_keys[1], (ROWS, HEADS, HD), 1.0, 5.0, ((0, 2), (1, 8)))
    new_value = scatter_about(part_keys[2], (ROWS, HEADS, HD), 3.0, 12.0, ((0, 2), (1, 8)))
    cache_keys = draw_cache_keys(jax.random.fold_in(jax.random.fold_in(arg_keys[8], part), 71), part)
    cache_values = draw_cache_values(jax.random.fold_in(jax.random.fold_in(arg_keys[8], part), 71), part)
    lengths = draw_lengths(jax.random.fold_in(jax.random.fold_in(arg_keys[8], part), 71), part)
    out_weight = bell_draw_with(arg_keys[6], (HEADS * HD, D), (HEADS * HD) ** -0.5, 0.25, ((0, 16),), (0, 1, 16, 2.0))
    residual = scatter_about(part_keys[7], (ROWS, D), 1.0, 6.0, ((1, 16),))
    return dict(query=query, new_key=new_key, new_value=new_value, cache_keys=cache_keys, cache_values=cache_values, lengths=lengths, out_weight=out_weight, residual=residual)


def reference(query, new_key, new_value, cache_keys, cache_values, lengths, out_weight, residual):
    scale = 1.0 / math.sqrt(HD)
    valid = jnp.arange(CTX)[None, :] < lengths[:, None]

    def head_context(items):
        q_head, k_new, v_new, keys, values = items
        q_float = q_head.astype(jnp.float32)
        scores = jnp.einsum('rd,rpd->rp', q_float, keys.astype(jnp.float32)) * scale
        own = lax.optimization_barrier(jnp.sum(q_float * k_new.astype(jnp.float32), axis=-1)) * scale
        scores = jnp.where(valid, scores, -jnp.inf)
        top = jnp.maximum(lax.optimization_barrier(jnp.max(scores, axis=-1)), own)
        expo = jnp.exp(scores - top[:, None])
        expo_own = jnp.exp(own - top)
        total = lax.optimization_barrier(jnp.sum(expo, axis=-1)) + expo_own
        probs = (expo / total[:, None]).astype(jnp.bfloat16)
        probs_own = (expo_own / total).astype(jnp.bfloat16)
        mixed = jnp.einsum('rp,rpd->rd', probs.astype(jnp.float32), values.astype(jnp.float32))
        mixed = mixed + probs_own.astype(jnp.float32)[:, None] * v_new.astype(jnp.float32)
        return mixed.astype(jnp.bfloat16)
    contexts = lax.map(head_context, (jnp.transpose(query, (1, 0, 2)), jnp.transpose(new_key, (1, 0, 2)), jnp.transpose(new_value, (1, 0, 2)), cache_keys, cache_values))
    context = jnp.transpose(contexts, (1, 0, 2)).reshape(ROWS, HEADS * HD)
    group = HEAD_DEV * HD // N_SUB
    groups = HEADS * HD // group
    context_groups = jnp.transpose(context.reshape(ROWS, groups, group), (1, 0, 2))
    weight_groups = out_weight.reshape(groups, group, D)

    def add_term(total, pair):
        piece, weights = pair
        return (total + jnp.dot(piece, weights, preferred_element_type=jnp.float32), None)
    attended, _ = lax.scan(add_term, jnp.zeros((ROWS, D), jnp.float32), (context_groups, weight_groups))
    return (residual.astype(jnp.float32) + attended).astype(jnp.bfloat16)
```

```python
import functools
import math

import jax
import jax.numpy as jnp
from jax import lax
from jax.experimental import pallas as pl
from jax.experimental.pallas import tpu as pltpu
from jax.sharding import PartitionSpec as P

D = 16384
INNER = 2
MESH = pl.DeviceIdType.MESH


def fused_kernel(
    outer,
    order,
    query_ref,
    key_ref,
    value_ref,
    lengths_ref,
    residual_ref,
    keys_hbm,
    values_hbm,
    weight_hbm,
    out_ref,
    keys,
    values,
    weight,
    context,
    x_out,
    x_in,
    z_out,
    z_in,
    totals,
    local_sem,
    weight_local,
    weight_send,
    weight_recv,
    context_sem,
    x_send,
    x_recv,
    z_send,
    z_recv,
    gz_send,
    gz_recv,
    gx_send,
    gx_recv,
    gs_send,
    gs_recv,
):
    tp = lax.axis_index("tp")
    sub = lax.axis_index("sub")
    z = lax.div(tp, INNER)
    x = lax.rem(tp, INNER)
    rows, head_dim = query_ref.shape
    all_rows, width = residual_ref.shape
    depth = weight_hbm.shape[0]
    slots = keys.shape[0] // rows

    other_core = {"sub": 1 - sub}
    other_x = {"tp": z * INNER + 1 - x}

    def along(k):
        return {"tp": lax.rem(z + k, outer) * INNER + x}

    def block_at(z_at, x_at, sub_at):
        first = ((z_at * INNER + x_at) * 2 + sub_at) * width
        return pl.ds(pl.multiple_of(first, width), width)

    barrier = pltpu.get_barrier_semaphore()
    partners = [other_core, other_x] + [along(k) for k in range(1, outer)]
    for partner in partners:
        pl.semaphore_signal(barrier, inc=1, device_id=partner, device_id_type=MESH)

    load_keys = pltpu.make_async_copy(keys_hbm, keys, local_sem.at[0])
    load_values = pltpu.make_async_copy(values_hbm, values, local_sem.at[1])
    load_keys.start()
    load_values.start()

    blocks = [(1 - x, k) for k in order] + [(x, k) for k in order]
    mine = pl.ds(pl.multiple_of(sub * depth, depth), depth)
    load_weight = []
    for j, (x_at, k) in enumerate(blocks):
        copy = pltpu.make_async_copy(
            weight_hbm.at[:, block_at(lax.rem(z + k, outer), x_at, sub)],
            weight.at[j, mine],
            weight_local.at[j],
        )
        copy.start()
        load_weight.append(copy)

    pl.semaphore_wait(barrier, len(partners))

    send_weight = []
    for j, (x_at, k) in enumerate(blocks):
        copy = pltpu.make_async_remote_copy(
            src_ref=weight_hbm.at[:, block_at(lax.rem(z + k, outer), x_at, 1 - sub)],
            dst_ref=weight.at[j, mine],
            send_sem=weight_send.at[j],
            recv_sem=weight_recv.at[j],
            device_id=other_core,
            device_id_type=MESH,
        )
        copy.start()
        send_weight.append(copy)

    scale = 1.0 / math.sqrt(head_dim)
    query = query_ref[...]
    row = lax.broadcasted_iota(jnp.int32, (rows, 1), 0)
    filled = jnp.zeros((rows, 1), jnp.int32)
    for r in range(rows):
        filled = jnp.where(row == r, lengths_ref[r], filled)
    own = (
        jnp.sum(
            query.astype(jnp.float32) * key_ref[...].astype(jnp.float32), axis=1, keepdims=True
        )
        * scale
    )
    load_keys.wait()
    scores = (
        lax.dot_general(
            query, keys[...], (((1,), (1,)), ((), ())), preferred_element_type=jnp.float32
        )
        * scale
    )
    place = lax.broadcasted_iota(jnp.int32, scores.shape, 1) - row * slots
    valid = (place >= 0) & (place < filled)
    scores = jnp.where(valid, scores, -jnp.inf)
    top = jnp.maximum(jnp.max(scores, axis=1, keepdims=True), own)
    expo = jnp.exp(scores - top)
    expo_own = jnp.exp(own - top)
    total = jnp.sum(expo, axis=1, keepdims=True) + expo_own
    probs = (expo / total).astype(jnp.bfloat16)
    probs_own = (expo_own / total).astype(jnp.bfloat16)
    load_values.wait()
    mixed = jnp.dot(probs, values[...], preferred_element_type=jnp.float32)
    mixed = mixed + probs_own.astype(jnp.float32) * value_ref[...].astype(jnp.float32)
    my_rows = pl.ds(pl.multiple_of(sub * rows, rows), rows)
    context[my_rows, :] = mixed.astype(jnp.bfloat16)
    send_context = pltpu.make_async_remote_copy(
        src_ref=context.at[my_rows],
        dst_ref=context.at[my_rows],
        send_sem=context_sem.at[0],
        recv_sem=context_sem.at[1],
        device_id=other_core,
        device_id_type=MESH,
    )
    send_context.start()
    send_context.wait_recv()
    whole_context = context[...]

    n = len(order)
    x_copies = []
    for j in range(n):
        load_weight[j].wait()
        send_weight[j].wait_recv()
        x_out[j] = jnp.dot(
            whole_context, weight[j], preferred_element_type=jnp.float32
        ).astype(jnp.bfloat16)
        copy = pltpu.make_async_remote_copy(
            src_ref=x_out.at[j],
            dst_ref=x_in.at[j],
            send_sem=x_send.at[j],
            recv_sem=x_recv.at[j],
            device_id=other_x,
            device_id_type=MESH,
        )
        copy.start()
        x_copies.append(copy)
    for j in range(n):
        load_weight[n + j].wait()
        send_weight[n + j].wait_recv()
        totals[j] = jnp.dot(whole_context, weight[n + j], preferred_element_type=jnp.float32)
    z_copies = {}
    summed = None
    for j, k in enumerate(order):
        x_copies[j].wait_recv()
        both = totals[j] + x_in[j].astype(jnp.float32)
        if k == 0:
            summed = both
            continue
        z_out[k - 1] = both.astype(jnp.bfloat16)
        copy = pltpu.make_async_remote_copy(
            src_ref=z_out.at[k - 1],
            dst_ref=z_in.at[k - 1],
            send_sem=z_send.at[k - 1],
            recv_sem=z_recv.at[k - 1],
            device_id=along(k),
            device_id_type=MESH,
        )
        copy.start()
        z_copies[k] = copy
    summed = summed + residual_ref[...].astype(jnp.float32)
    for k in order:
        if k > 0:
            z_copies[k].wait_recv()
            summed = summed + z_in[k - 1].astype(jnp.float32)
    here = block_at(z, x, sub)
    out_ref[:, here] = summed.astype(jnp.bfloat16)

    sent = []

    def pass_on(block, device, send_sem, recv_sem):
        copy = pltpu.make_async_remote_copy(
            src_ref=out_ref.at[:, block],
            dst_ref=out_ref.at[:, block],
            send_sem=send_sem,
            recv_sem=recv_sem,
            device_id=device,
            device_id_type=MESH,
        )
        copy.start()
        sent.append(copy)
        return copy

    def arrived(block, send_sem, recv_sem):
        pltpu.make_async_remote_copy(
            src_ref=out_ref.at[:, block],
            dst_ref=out_ref.at[:, block],
            send_sem=send_sem,
            recv_sem=recv_sem,
            device_id=other_core,
            device_id_type=MESH,
        ).wait_recv()

    hops = [0] + [k for k in order if k > 0]
    for k in hops[1:]:
        pass_on(here, along(k), gz_send.at[k - 1], gz_recv.at[k - 1])
    for k in hops:
        block = block_at(lax.rem(z + outer - k, outer), x, sub)
        if k > 0:
            arrived(block, gz_send.at[k - 1], gz_recv.at[k - 1])
        pass_on(block, other_x, gx_send.at[k], gx_recv.at[k])
        pass_on(block, other_core, gs_send.at[k], gs_recv.at[k])
    for k in hops:
        block = block_at(lax.rem(z + outer - k, outer), 1 - x, sub)
        arrived(block, gx_send.at[k], gx_recv.at[k])
        pass_on(block, other_core, gs_send.at[outer + k], gs_recv.at[outer + k])
    for i, x_at in enumerate((x, 1 - x)):
        for k in hops:
            block = block_at(lax.rem(z + outer - k, outer), x_at, 1 - sub)
            arrived(block, gs_send.at[i * outer + k], gs_recv.at[i * outer + k])

    send_context.wait_send()
    for copy in send_weight + x_copies + list(z_copies.values()) + sent:
        copy.wait_send()


def per_device_fused(
    query, new_key, new_value, cache_keys, cache_values, lengths, out_weight, residual
):
    rows, _, head_dim = query.shape
    slots = cache_keys.shape[2]
    depth, columns = out_weight.shape
    all_rows, width = residual.shape
    outer = lax.axis_size("tp") // INNER
    order = [2, 1, 3, 0] if outer == 4 else [k for k in range(1, outer)] + [0]
    vmem = pl.BlockSpec(memory_space=pltpu.VMEM)
    anywhere = pl.BlockSpec(memory_space=pl.ANY)
    block = (all_rows, width)
    dma = pltpu.SemaphoreType.DMA
    return pl.pallas_call(
        functools.partial(fused_kernel, outer, order),
        out_shape=jax.ShapeDtypeStruct((all_rows, columns), jnp.bfloat16),
        in_specs=[vmem] * 3
        + [pl.BlockSpec(memory_space=pltpu.SMEM), vmem]
        + [anywhere] * 3,
        out_specs=vmem,
        scratch_shapes=[
            pltpu.VMEM((rows * slots, head_dim), jnp.bfloat16),
            pltpu.VMEM((rows * slots, head_dim), jnp.bfloat16),
            pltpu.VMEM((2 * outer, 2 * depth, width), jnp.bfloat16),
            pltpu.VMEM((all_rows, head_dim), jnp.bfloat16),
            pltpu.VMEM((outer, *block), jnp.bfloat16),
            pltpu.VMEM((outer, *block), jnp.bfloat16),
            pltpu.VMEM((outer - 1, *block), jnp.bfloat16),
            pltpu.VMEM((outer - 1, *block), jnp.bfloat16),
            pltpu.VMEM((outer, *block), jnp.float32),
            dma((2,)),
            dma((2 * outer,)),
            dma((2 * outer,)),
            dma((2 * outer,)),
            dma((2,)),
            dma((outer,)),
            dma((outer,)),
            dma((outer - 1,)),
            dma((outer - 1,)),
            dma((outer - 1,)),
            dma((outer - 1,)),
            dma((outer,)),
            dma((outer,)),
            dma((2 * outer,)),
            dma((2 * outer,)),
        ],
        compiler_params=pltpu.CompilerParams(
            collective_id=0, has_side_effects=True, vmem_limit_bytes=56 * 2**20
        ),
    )(
        query.reshape(rows, head_dim),
        new_key.reshape(rows, head_dim),
        new_value.reshape(rows, head_dim),
        lengths,
        residual,
        cache_keys.reshape(rows * slots, head_dim),
        cache_values.reshape(rows * slots, head_dim),
        out_weight,
    )


def per_device(query, new_key, new_value, cache_keys, cache_values, lengths, out_weight, residual):
    rows_here, heads_here, head_dim = query.shape
    slots = cache_keys.shape[2]
    scale = 1.0 / math.sqrt(head_dim)
    scores = (
        jnp.einsum("rhd,hrpd->hrp", query, cache_keys, preferred_element_type=jnp.float32) * scale
    )
    own = jnp.sum(query.astype(jnp.float32) * new_key.astype(jnp.float32), axis=-1) * scale
    own = jnp.transpose(own)
    valid = jnp.arange(slots)[None, None, :] < lengths[None, :, None]
    scores = jnp.where(valid, scores, -jnp.inf)
    top = jnp.maximum(jnp.max(scores, axis=-1), own)
    expo = jnp.exp(scores - top[:, :, None])
    expo_own = jnp.exp(own - top)
    total = jnp.sum(expo, axis=-1) + expo_own
    probs = (expo / total[:, :, None]).astype(jnp.bfloat16)
    probs_own = (expo_own / total).astype(jnp.bfloat16)
    mixed = jnp.einsum("hrp,hrpd->rhd", probs, cache_values, preferred_element_type=jnp.float32)
    mixed = mixed + jnp.transpose(probs_own).astype(jnp.float32)[:, :, None] * new_value.astype(
        jnp.float32
    )
    context = mixed.astype(jnp.bfloat16).reshape(rows_here, heads_here * head_dim)
    halves = lax.all_to_all(context, "sub", split_axis=1, concat_axis=0, tiled=True)
    all_rows = halves.shape[0]
    n_tp = lax.axis_size("tp")
    n_sub = lax.axis_size("sub")
    n_all = n_tp * n_sub
    width = D // n_all
    weight_view = out_weight.reshape(out_weight.shape[0], n_all, width)
    partial_value = jnp.einsum(
        "rk,kgc->grc", halves, weight_view, preferred_element_type=jnp.float32
    )
    arranged = partial_value.reshape(n_all, all_rows * width)
    summed = lax.psum_scatter(arranged, ("tp", "sub"), scatter_dimension=0, tiled=True)
    own_columns = summed.reshape(all_rows, width)
    updated = (residual.astype(jnp.float32) + own_columns).astype(jnp.bfloat16)
    gathered = lax.all_gather(
        updated.reshape(1, all_rows * width), ("tp", "sub"), axis=0, tiled=True
    )
    whole = jnp.transpose(gathered.reshape(n_all, all_rows, width), (1, 0, 2))
    return whole.reshape(all_rows, D)


def solution(mesh):
    n_tp, n_sub = mesh.shape["tp"], mesh.shape["sub"]
    width = D // (n_tp * n_sub)
    fused = n_sub == 2 and n_tp % INNER == 0 and 4 <= n_tp <= 16 and width % 128 == 0
    return jax.shard_map(
        per_device_fused if fused else per_device,
        mesh=mesh,
        in_specs=(
            P(("rep", "sub"), "tp", None),
            P(("rep", "sub"), "tp", None),
            P(("rep", "sub"), "tp", None),
            P("tp", ("rep", "sub"), None, None),
            P("tp", ("rep", "sub"), None, None),
            P(("rep", "sub")),
            P(("tp", "sub"), None),
            P("rep", ("tp", "sub")),
        ),
        out_specs=P("rep", None),
        check_vma=False,
    )
```

```python
import functools
import math

import jax
import jax.numpy as jnp
from jax import lax
from jax.experimental import pallas as pl
from jax.experimental.pallas import tpu as pltpu
from jax.sharding import PartitionSpec as P

D = 16384
INNER = 2
PARTS = 2
MESH = pl.DeviceIdType.MESH


def fused_kernel(
    outer,
    order,
    query_ref,
    key_ref,
    value_ref,
    lengths_ref,
    residual_ref,
    keys_hbm,
    values_hbm,
    weight_hbm,
    out_ref,
    keys,
    values,
    weight,
    context,
    x_out,
    x_in,
    z_out,
    z_in,
    totals,
    local_sem,
    weight_local,
    weight_send,
    weight_recv,
    context_sem,
    x_send,
    x_recv,
    z_send,
    z_recv,
    gz_send,
    gz_recv,
    gx_send,
    gx_recv,
    gs_send,
    gs_recv,
):
    tp = lax.axis_index("tp")
    sub = lax.axis_index("sub")
    z = lax.div(tp, INNER)
    x = lax.rem(tp, INNER)
    rows, head_dim = query_ref.shape
    all_rows, width = residual_ref.shape
    depth = weight_hbm.shape[0]
    slots = keys.shape[0] // rows

    other_core = {"sub": 1 - sub}
    other_x = {"tp": z * INNER + 1 - x}

    def along(k):
        return {"tp": lax.rem(z + k, outer) * INNER + x}

    def block_at(z_at, x_at, sub_at):
        first = ((z_at * INNER + x_at) * 2 + sub_at) * width
        return pl.ds(pl.multiple_of(first, width), width)

    barrier = pltpu.get_barrier_semaphore()
    partners = [other_core, other_x] + [along(k) for k in range(1, outer)]
    for partner in partners:
        pl.semaphore_signal(barrier, inc=1, device_id=partner, device_id_type=MESH)

    load_keys = pltpu.make_async_copy(keys_hbm, keys, local_sem.at[0])
    load_values = pltpu.make_async_copy(values_hbm, values, local_sem.at[1])
    load_keys.start()
    load_values.start()

    blocks = [(1 - x, k) for k in order] + [(x, k) for k in order]
    mine = pl.ds(pl.multiple_of(sub * depth, depth), depth)
    load_weight = []
    for j, (x_at, k) in enumerate(blocks):
        copy = pltpu.make_async_copy(
            weight_hbm.at[:, block_at(lax.rem(z + k, outer), x_at, sub)],
            weight.at[j, mine],
            weight_local.at[j],
        )
        copy.start()
        load_weight.append(copy)

    scale = 1.0 / math.sqrt(head_dim)
    query = query_ref[...]
    row = lax.broadcasted_iota(jnp.int32, (rows, 1), 0)
    filled = jnp.zeros((rows, 1), jnp.int32)
    for r in range(rows):
        filled = jnp.where(row == r, lengths_ref[r], filled)
    own = (
        jnp.sum(
            query.astype(jnp.float32) * key_ref[...].astype(jnp.float32), axis=1, keepdims=True
        )
        * scale
    )
    load_keys.wait()
    scores = (
        lax.dot_general(
            query, keys[...], (((1,), (1,)), ((), ())), preferred_element_type=jnp.float32
        )
        * scale
    )
    pl.semaphore_wait(barrier, len(partners))

    send_weight = []
    for j, (x_at, k) in enumerate(blocks):
        copy = pltpu.make_async_remote_copy(
            src_ref=weight_hbm.at[:, block_at(lax.rem(z + k, outer), x_at, 1 - sub)],
            dst_ref=weight.at[j, mine],
            send_sem=weight_send.at[j],
            recv_sem=weight_recv.at[j],
            device_id=other_core,
            device_id_type=MESH,
        )
        copy.start()
        send_weight.append(copy)

    place = lax.broadcasted_iota(jnp.int32, scores.shape, 1) - row * slots
    valid = (place >= 0) & (place < filled)
    scores = jnp.where(valid, scores, -jnp.inf)
    top = jnp.maximum(jnp.max(scores, axis=1, keepdims=True), own)
    expo = jnp.exp(scores - top)
    expo_own = jnp.exp(own - top)
    total = jnp.sum(expo, axis=1, keepdims=True) + expo_own
    probs = (expo / total).astype(jnp.bfloat16)
    probs_own = (expo_own / total).astype(jnp.bfloat16)
    load_values.wait()
    mixed = jnp.dot(probs, values[...], preferred_element_type=jnp.float32)
    mixed = mixed + probs_own.astype(jnp.float32) * value_ref[...].astype(jnp.float32)
    my_rows = pl.ds(pl.multiple_of(sub * rows, rows), rows)
    context[my_rows, :] = mixed.astype(jnp.bfloat16)
    send_context = pltpu.make_async_remote_copy(
        src_ref=context.at[my_rows],
        dst_ref=context.at[my_rows],
        send_sem=context_sem.at[0],
        recv_sem=context_sem.at[1],
        device_id=other_core,
        device_id_type=MESH,
    )
    send_context.start()
    send_context.wait_recv()
    whole_context = context[...]

    n = len(order)
    part = width // PARTS
    parts = [slice(p * part, (p + 1) * part) for p in range(PARTS)]
    sent = []

    def send(src, dst, device, send_sem, recv_sem):
        copy = pltpu.make_async_remote_copy(
            src_ref=src,
            dst_ref=dst,
            send_sem=send_sem,
            recv_sem=recv_sem,
            device_id=device,
            device_id_type=MESH,
        )
        copy.start()
        sent.append(copy)
        return copy

    x_copies = {}
    for p, cols in enumerate(parts):
        for j in range(n):
            if p == 0:
                load_weight[j].wait()
                send_weight[j].wait_recv()
            x_out[j, :, cols] = jnp.dot(
                whole_context, weight[j, :, cols], preferred_element_type=jnp.float32
            ).astype(jnp.bfloat16)
            x_copies[p, j] = send(
                x_out.at[j, :, cols],
                x_in.at[j, :, cols],
                other_x,
                x_send.at[p, j],
                x_recv.at[p, j],
            )
    for j in range(n):
        load_weight[n + j].wait()
        send_weight[n + j].wait_recv()
        totals[j] = jnp.dot(whole_context, weight[n + j], preferred_element_type=jnp.float32)
    z_copies = {}
    for p, cols in enumerate(parts):
        for j, k in enumerate(order):
            x_copies[p, j].wait_recv()
            both = totals[j, :, cols] + x_in[j, :, cols].astype(jnp.float32)
            if k == 0:
                totals[j, :, cols] = both
                continue
            z_out[k - 1, :, cols] = both.astype(jnp.bfloat16)
            z_copies[p, k] = send(
                z_out.at[k - 1, :, cols],
                z_in.at[k - 1, :, cols],
                along(k),
                z_send.at[p, k - 1],
                z_recv.at[p, k - 1],
            )

    hops = [0] + sorted([k for k in order if k > 0], key=lambda k: min(k, outer - k))

    def piece_at(k, x_at, sub_at, p):
        at = lax.rem(z + outer - k, outer)
        first = ((at * INNER + x_at) * 2 + sub_at) * width + p * part
        return out_ref.at[:, pl.ds(pl.multiple_of(first, part), part)]

    along_z = {}
    along_x = {}
    across = {}
    for p, cols in enumerate(parts):
        summed = totals[n - 1, :, cols] + residual_ref[:, cols].astype(jnp.float32)
        for k in order:
            if k > 0:
                z_copies[p, k].wait_recv()
                summed = summed + z_in[k - 1, :, cols].astype(jnp.float32)
        here = piece_at(0, x, sub, p)
        here[...] = summed.astype(jnp.bfloat16)
        along_x[p, 0] = send(here, here, other_x, gx_send.at[p, 0], gx_recv.at[p, 0])
        across[p, 0] = send(here, here, other_core, gs_send.at[p, 0], gs_recv.at[p, 0])
        for k in hops[1:]:
            along_z[p, k] = send(
                here, here, along(k), gz_send.at[p, k - 1], gz_recv.at[p, k - 1]
            )
    for p in range(PARTS):
        for k in hops[1:]:
            along_z[p, k].wait_recv()
            piece = piece_at(k, x, sub, p)
            along_x[p, k] = send(piece, piece, other_x, gx_send.at[p, k], gx_recv.at[p, k])
            across[p, k] = send(piece, piece, other_core, gs_send.at[p, k], gs_recv.at[p, k])
    for p in range(PARTS):
        for k in hops:
            along_x[p, k].wait_recv()
            piece = piece_at(k, 1 - x, sub, p)
            i = outer + k
            across[p, i] = send(piece, piece, other_core, gs_send.at[p, i], gs_recv.at[p, i])
    for copy in across.values():
        copy.wait_recv()
    send_context.wait_send()
    for copy in send_weight + sent:
        copy.wait_send()


def per_device_fused(
    query, new_key, new_value, cache_keys, cache_values, lengths, out_weight, residual
):
    rows, _, head_dim = query.shape
    slots = cache_keys.shape[2]
    depth, columns = out_weight.shape
    all_rows, width = residual.shape
    outer = lax.axis_size("tp") // INNER
    order = [2, 1, 3, 0] if outer == 4 else [k for k in range(1, outer)] + [0]
    vmem = pl.BlockSpec(memory_space=pltpu.VMEM)
    anywhere = pl.BlockSpec(memory_space=pl.ANY)
    block = (all_rows, width)
    dma = pltpu.SemaphoreType.DMA
    return pl.pallas_call(
        functools.partial(fused_kernel, outer, order),
        out_shape=jax.ShapeDtypeStruct((all_rows, columns), jnp.bfloat16),
        in_specs=[vmem] * 3
        + [pl.BlockSpec(memory_space=pltpu.SMEM), vmem]
        + [anywhere] * 3,
        out_specs=vmem,
        scratch_shapes=[
            pltpu.VMEM((rows * slots, head_dim), jnp.bfloat16),
            pltpu.VMEM((rows * slots, head_dim), jnp.bfloat16),
            pltpu.VMEM((2 * outer, 2 * depth, width), jnp.bfloat16),
            pltpu.VMEM((all_rows, head_dim), jnp.bfloat16),
            pltpu.VMEM((outer, *block), jnp.bfloat16),
            pltpu.VMEM((outer, *block), jnp.bfloat16),
            pltpu.VMEM((outer - 1, *block), jnp.bfloat16),
            pltpu.VMEM((outer - 1, *block), jnp.bfloat16),
            pltpu.VMEM((outer, *block), jnp.float32),
            dma((2,)),
            dma((2 * outer,)),
            dma((2 * outer,)),
            dma((2 * outer,)),
            dma((2,)),
            dma((PARTS, outer)),
            dma((PARTS, outer)),
            dma((PARTS, outer - 1)),
            dma((PARTS, outer - 1)),
            dma((PARTS, outer - 1)),
            dma((PARTS, outer - 1)),
            dma((PARTS, outer)),
            dma((PARTS, outer)),
            dma((PARTS, 2 * outer)),
            dma((PARTS, 2 * outer)),
        ],
        compiler_params=pltpu.CompilerParams(
            collective_id=0, has_side_effects=True, vmem_limit_bytes=56 * 2**20
        ),
    )(
        query.reshape(rows, head_dim),
        new_key.reshape(rows, head_dim),
        new_value.reshape(rows, head_dim),
        lengths,
        residual,
        cache_keys.reshape(rows * slots, head_dim),
        cache_values.reshape(rows * slots, head_dim),
        out_weight,
    )


def per_device(query, new_key, new_value, cache_keys, cache_values, lengths, out_weight, residual):
    rows_here, heads_here, head_dim = query.shape
    slots = cache_keys.shape[2]
    scale = 1.0 / math.sqrt(head_dim)
    scores = (
        jnp.einsum("rhd,hrpd->hrp", query, cache_keys, preferred_element_type=jnp.float32) * scale
    )
    own = jnp.sum(query.astype(jnp.float32) * new_key.astype(jnp.float32), axis=-1) * scale
    own = jnp.transpose(own)
    valid = jnp.arange(slots)[None, None, :] < lengths[None, :, None]
    scores = jnp.where(valid, scores, -jnp.inf)
    top = jnp.maximum(jnp.max(scores, axis=-1), own)
    expo = jnp.exp(scores - top[:, :, None])
    expo_own = jnp.exp(own - top)
    total = jnp.sum(expo, axis=-1) + expo_own
    probs = (expo / total[:, :, None]).astype(jnp.bfloat16)
    probs_own = (expo_own / total).astype(jnp.bfloat16)
    mixed = jnp.einsum("hrp,hrpd->rhd", probs, cache_values, preferred_element_type=jnp.float32)
    mixed = mixed + jnp.transpose(probs_own).astype(jnp.float32)[:, :, None] * new_value.astype(
        jnp.float32
    )
    context = mixed.astype(jnp.bfloat16).reshape(rows_here, heads_here * head_dim)
    halves = lax.all_to_all(context, "sub", split_axis=1, concat_axis=0, tiled=True)
    all_rows = halves.shape[0]
    n_tp = lax.axis_size("tp")
    n_sub = lax.axis_size("sub")
    n_all = n_tp * n_sub
    width = D // n_all
    weight_view = out_weight.reshape(out_weight.shape[0], n_all, width)
    partial_value = jnp.einsum(
        "rk,kgc->grc", halves, weight_view, preferred_element_type=jnp.float32
    )
    arranged = partial_value.reshape(n_all, all_rows * width)
    summed = lax.psum_scatter(arranged, ("tp", "sub"), scatter_dimension=0, tiled=True)
    own_columns = summed.reshape(all_rows, width)
    updated = (residual.astype(jnp.float32) + own_columns).astype(jnp.bfloat16)
    gathered = lax.all_gather(
        updated.reshape(1, all_rows * width), ("tp", "sub"), axis=0, tiled=True
    )
    whole = jnp.transpose(gathered.reshape(n_all, all_rows, width), (1, 0, 2))
    return whole.reshape(all_rows, D)


def solution(mesh):
    n_tp, n_sub = mesh.shape["tp"], mesh.shape["sub"]
    width = D // (n_tp * n_sub)
    fused = n_sub == 2 and n_tp % INNER == 0 and 4 <= n_tp <= 16 and width % (128 * PARTS) == 0
    return jax.shard_map(
        per_device_fused if fused else per_device,
        mesh=mesh,
        in_specs=(
            P(("rep", "sub"), "tp", None),
            P(("rep", "sub"), "tp", None),
            P(("rep", "sub"), "tp", None),
            P("tp", ("rep", "sub"), None, None),
            P("tp", ("rep", "sub"), None, None),
            P(("rep", "sub")),
            P(("tp", "sub"), None),
            P("rep", ("tp", "sub")),
        ),
        out_specs=P("rep", None),
        check_vma=False,
    )
```

```python
import functools
import math

import jax
import jax.numpy as jnp
from jax import lax
from jax.experimental import pallas as pl
from jax.experimental.pallas import tpu as pltpu
from jax.sharding import PartitionSpec as P

D = 16384
INNER = 2
PARTS = 2
MESH = pl.DeviceIdType.MESH


def fused_kernel(
    outer,
    order,
    query_ref,
    key_ref,
    value_ref,
    lengths_ref,
    residual_ref,
    keys_hbm,
    values_hbm,
    weight_hbm,
    out_ref,
    keys,
    values,
    weight,
    context,
    x_out,
    x_in,
    z_out,
    z_in,
    totals,
    local_sem,
    weight_local,
    weight_send,
    weight_recv,
    context_sem,
    x_send,
    x_recv,
    z_send,
    z_recv,
    gz_send,
    gz_recv,
    gx_send,
    gx_recv,
    gs_send,
    gs_recv,
):
    tp = lax.axis_index("tp")
    sub = lax.axis_index("sub")
    z = lax.div(tp, INNER)
    x = lax.rem(tp, INNER)
    rows, head_dim = query_ref.shape
    all_rows, width = residual_ref.shape
    depth = weight_hbm.shape[0]
    slots = keys.shape[0] // rows

    other_core = {"sub": 1 - sub}
    other_x = {"tp": z * INNER + 1 - x}

    def along(k):
        return {"tp": lax.rem(z + k, outer) * INNER + x}

    def block_at(z_at, x_at, sub_at):
        first = ((z_at * INNER + x_at) * 2 + sub_at) * width
        return pl.ds(pl.multiple_of(first, width), width)

    barrier = pltpu.get_barrier_semaphore()
    partners = [other_core, other_x] + [along(k) for k in range(1, outer)]
    for partner in partners:
        pl.semaphore_signal(barrier, inc=1, device_id=partner, device_id_type=MESH)

    load_keys = pltpu.make_async_copy(keys_hbm, keys, local_sem.at[0])
    load_values = pltpu.make_async_copy(values_hbm, values, local_sem.at[1])
    load_keys.start()
    load_values.start()

    blocks = [(1 - x, k) for k in order] + [(x, k) for k in order]
    mine = pl.ds(pl.multiple_of(sub * depth, depth), depth)
    load_weight = []
    for j, (x_at, k) in enumerate(blocks):
        copy = pltpu.make_async_copy(
            weight_hbm.at[:, block_at(lax.rem(z + k, outer), x_at, sub)],
            weight.at[j, mine],
            weight_local.at[j],
        )
        copy.start()
        load_weight.append(copy)

    scale = 1.0 / math.sqrt(head_dim)
    query = query_ref[...]
    row = lax.broadcasted_iota(jnp.int32, (rows, 1), 0)
    filled = jnp.zeros((rows, 1), jnp.int32)
    for r in range(rows):
        filled = jnp.where(row == r, lengths_ref[r], filled)
    own = (
        jnp.sum(
            query.astype(jnp.float32) * key_ref[...].astype(jnp.float32), axis=1, keepdims=True
        )
        * scale
    )
    load_keys.wait()
    scores = (
        lax.dot_general(
            query, keys[...], (((1,), (1,)), ((), ())), preferred_element_type=jnp.float32
        )
        * scale
    )
    place = lax.broadcasted_iota(jnp.int32, scores.shape, 1) - row * slots
    valid = (place >= 0) & (place < filled)
    scores = jnp.where(valid, scores, -jnp.inf)
    top = jnp.maximum(jnp.max(scores, axis=1, keepdims=True), own)
    expo = jnp.exp(scores - top)
    expo_own = jnp.exp(own - top)
    total = jnp.sum(expo, axis=1, keepdims=True) + expo_own
    probs = (expo / total).astype(jnp.bfloat16)
    probs_own = (expo_own / total).astype(jnp.bfloat16)
    pl.semaphore_wait(barrier, len(partners))

    send_weight = []
    for j, (x_at, k) in enumerate(blocks):
        copy = pltpu.make_async_remote_copy(
            src_ref=weight_hbm.at[:, block_at(lax.rem(z + k, outer), x_at, 1 - sub)],
            dst_ref=weight.at[j, mine],
            send_sem=weight_send.at[j],
            recv_sem=weight_recv.at[j],
            device_id=other_core,
            device_id_type=MESH,
        )
        copy.start()
        send_weight.append(copy)

    load_values.wait()
    mixed = jnp.dot(probs, values[...], preferred_element_type=jnp.float32)
    mixed = mixed + probs_own.astype(jnp.float32) * value_ref[...].astype(jnp.float32)
    my_rows = pl.ds(pl.multiple_of(sub * rows, rows), rows)
    context[my_rows, :] = mixed.astype(jnp.bfloat16)
    send_context = pltpu.make_async_remote_copy(
        src_ref=context.at[my_rows],
        dst_ref=context.at[my_rows],
        send_sem=context_sem.at[0],
        recv_sem=context_sem.at[1],
        device_id=other_core,
        device_id_type=MESH,
    )
    send_context.start()
    send_context.wait_recv()
    whole_context = context[...]

    n = len(order)
    part = width // PARTS
    parts = [slice(p * part, (p + 1) * part) for p in range(PARTS)]
    sent = []

    def send(src, dst, device, send_sem, recv_sem):
        copy = pltpu.make_async_remote_copy(
            src_ref=src,
            dst_ref=dst,
            send_sem=send_sem,
            recv_sem=recv_sem,
            device_id=device,
            device_id_type=MESH,
        )
        copy.start()
        sent.append(copy)
        return copy

    x_copies = {}
    for p, cols in enumerate(parts):
        for j in range(n):
            if p == 0:
                load_weight[j].wait()
                send_weight[j].wait_recv()
            x_out[j, :, cols] = jnp.dot(
                whole_context, weight[j, :, cols], preferred_element_type=jnp.float32
            ).astype(jnp.bfloat16)
            x_copies[p, j] = send(
                x_out.at[j, :, cols],
                x_in.at[j, :, cols],
                other_x,
                x_send.at[p, j],
                x_recv.at[p, j],
            )
    for j in range(n):
        load_weight[n + j].wait()
        send_weight[n + j].wait_recv()
        totals[j] = jnp.dot(whole_context, weight[n + j], preferred_element_type=jnp.float32)
    z_copies = {}
    for p, cols in enumerate(parts):
        for j, k in enumerate(order):
            x_copies[p, j].wait_recv()
            both = totals[j, :, cols] + x_in[j, :, cols].astype(jnp.float32)
            if k == 0:
                totals[j, :, cols] = both
                continue
            z_out[k - 1, :, cols] = both.astype(jnp.bfloat16)
            z_copies[p, k] = send(
                z_out.at[k - 1, :, cols],
                z_in.at[k - 1, :, cols],
                along(k),
                z_send.at[p, k - 1],
                z_recv.at[p, k - 1],
            )

    hops = [0] + sorted([k for k in order if k > 0], key=lambda k: min(k, outer - k))

    def piece_at(k, x_at, sub_at, p):
        at = lax.rem(z + outer - k, outer)
        first = ((at * INNER + x_at) * 2 + sub_at) * width + p * part
        return out_ref.at[:, pl.ds(pl.multiple_of(first, part), part)]

    along_z = {}
    along_x = {}
    across = {}
    for p, cols in enumerate(parts):
        summed = totals[n - 1, :, cols] + residual_ref[:, cols].astype(jnp.float32)
        for k in order:
            if k > 0:
                z_copies[p, k].wait_recv()
                summed = summed + z_in[k - 1, :, cols].astype(jnp.float32)
        here = piece_at(0, x, sub, p)
        here[...] = summed.astype(jnp.bfloat16)
        along_x[p, 0] = send(here, here, other_x, gx_send.at[p, 0], gx_recv.at[p, 0])
        across[p, 0] = send(here, here, other_core, gs_send.at[p, 0], gs_recv.at[p, 0])
        for k in hops[1:]:
            along_z[p, k] = send(
                here, here, along(k), gz_send.at[p, k - 1], gz_recv.at[p, k - 1]
            )
    def from_z(p, k):
        along_z[p, k].wait_recv()
        piece = piece_at(k, x, sub, p)
        along_x[p, k] = send(piece, piece, other_x, gx_send.at[p, k], gx_recv.at[p, k])
        across[p, k] = send(piece, piece, other_core, gs_send.at[p, k], gs_recv.at[p, k])

    def from_x(p, k):
        along_x[p, k].wait_recv()
        piece = piece_at(k, 1 - x, sub, p)
        i = outer + k
        across[p, i] = send(piece, piece, other_core, gs_send.at[p, i], gs_recv.at[p, i])

    for p in range(PARTS + 1):
        for k in hops:
            if p < PARTS and k > 0:
                from_z(p, k)
            if p > 0:
                from_x(p - 1, k)
    for copy in across.values():
        copy.wait_recv()
    send_context.wait_send()
    for copy in send_weight + sent:
        copy.wait_send()


def per_device_fused(
    query, new_key, new_value, cache_keys, cache_values, lengths, out_weight, residual
):
    rows, _, head_dim = query.shape
    slots = cache_keys.shape[2]
    depth, columns = out_weight.shape
    all_rows, width = residual.shape
    outer = lax.axis_size("tp") // INNER
    order = [2, 1, 3, 0] if outer == 4 else [k for k in range(1, outer)] + [0]
    vmem = pl.BlockSpec(memory_space=pltpu.VMEM)
    anywhere = pl.BlockSpec(memory_space=pl.ANY)
    block = (all_rows, width)
    dma = pltpu.SemaphoreType.DMA
    return pl.pallas_call(
        functools.partial(fused_kernel, outer, order),
        out_shape=jax.ShapeDtypeStruct((all_rows, columns), jnp.bfloat16),
        in_specs=[vmem] * 3
        + [pl.BlockSpec(memory_space=pltpu.SMEM), vmem]
        + [anywhere] * 3,
        out_specs=vmem,
        scratch_shapes=[
            pltpu.VMEM((rows * slots, head_dim), jnp.bfloat16),
            pltpu.VMEM((rows * slots, head_dim), jnp.bfloat16),
            pltpu.VMEM((2 * outer, 2 * depth, width), jnp.bfloat16),
            pltpu.VMEM((all_rows, head_dim), jnp.bfloat16),
            pltpu.VMEM((outer, *block), jnp.bfloat16),
            pltpu.VMEM((outer, *block), jnp.bfloat16),
            pltpu.VMEM((outer - 1, *block), jnp.bfloat16),
            pltpu.VMEM((outer - 1, *block), jnp.bfloat16),
            pltpu.VMEM((outer, *block), jnp.float32),
            dma((2,)),
            dma((2 * outer,)),
            dma((2 * outer,)),
            dma((2 * outer,)),
            dma((2,)),
            dma((PARTS, outer)),
            dma((PARTS, outer)),
            dma((PARTS, outer - 1)),
            dma((PARTS, outer - 1)),
            dma((PARTS, outer - 1)),
            dma((PARTS, outer - 1)),
            dma((PARTS, outer)),
            dma((PARTS, outer)),
            dma((PARTS, 2 * outer)),
            dma((PARTS, 2 * outer)),
        ],
        compiler_params=pltpu.CompilerParams(
            collective_id=0, has_side_effects=True, vmem_limit_bytes=56 * 2**20
        ),
    )(
        query.reshape(rows, head_dim),
        new_key.reshape(rows, head_dim),
        new_value.reshape(rows, head_dim),
        lengths,
        residual,
        cache_keys.reshape(rows * slots, head_dim),
        cache_values.reshape(rows * slots, head_dim),
        out_weight,
    )


def per_device(query, new_key, new_value, cache_keys, cache_values, lengths, out_weight, residual):
    rows_here, heads_here, head_dim = query.shape
    slots = cache_keys.shape[2]
    scale = 1.0 / math.sqrt(head_dim)
    scores = (
        jnp.einsum("rhd,hrpd->hrp", query, cache_keys, preferred_element_type=jnp.float32) * scale
    )
    own = jnp.sum(query.astype(jnp.float32) * new_key.astype(jnp.float32), axis=-1) * scale
    own = jnp.transpose(own)
    valid = jnp.arange(slots)[None, None, :] < lengths[None, :, None]
    scores = jnp.where(valid, scores, -jnp.inf)
    top = jnp.maximum(jnp.max(scores, axis=-1), own)
    expo = jnp.exp(scores - top[:, :, None])
    expo_own = jnp.exp(own - top)
    total = jnp.sum(expo, axis=-1) + expo_own
    probs = (expo / total[:, :, None]).astype(jnp.bfloat16)
    probs_own = (expo_own / total).astype(jnp.bfloat16)
    mixed = jnp.einsum("hrp,hrpd->rhd", probs, cache_values, preferred_element_type=jnp.float32)
    mixed = mixed + jnp.transpose(probs_own).astype(jnp.float32)[:, :, None] * new_value.astype(
        jnp.float32
    )
    context = mixed.astype(jnp.bfloat16).reshape(rows_here, heads_here * head_dim)
    halves = lax.all_to_all(context, "sub", split_axis=1, concat_axis=0, tiled=True)
    all_rows = halves.shape[0]
    n_tp = lax.axis_size("tp")
    n_sub = lax.axis_size("sub")
    n_all = n_tp * n_sub
    width = D // n_all
    weight_view = out_weight.reshape(out_weight.shape[0], n_all, width)
    partial_value = jnp.einsum(
        "rk,kgc->grc", halves, weight_view, preferred_element_type=jnp.float32
    )
    arranged = partial_value.reshape(n_all, all_rows * width)
    summed = lax.psum_scatter(arranged, ("tp", "sub"), scatter_dimension=0, tiled=True)
    own_columns = summed.reshape(all_rows, width)
    updated = (residual.astype(jnp.float32) + own_columns).astype(jnp.bfloat16)
    gathered = lax.all_gather(
        updated.reshape(1, all_rows * width), ("tp", "sub"), axis=0, tiled=True
    )
    whole = jnp.transpose(gathered.reshape(n_all, all_rows, width), (1, 0, 2))
    return whole.reshape(all_rows, D)


def solution(mesh):
    n_tp, n_sub = mesh.shape["tp"], mesh.shape["sub"]
    width = D // (n_tp * n_sub)
    fused = n_sub == 2 and n_tp % INNER == 0 and 4 <= n_tp <= 16 and width % (128 * PARTS) == 0
    return jax.shard_map(
        per_device_fused if fused else per_device,
        mesh=mesh,
        in_specs=(
            P(("rep", "sub"), "tp", None),
            P(("rep", "sub"), "tp", None),
            P(("rep", "sub"), "tp", None),
            P("tp", ("rep", "sub"), None, None),
            P("tp", ("rep", "sub"), None, None),
            P(("rep", "sub")),
            P(("tp", "sub"), None),
            P("rep", ("tp", "sub")),
        ),
        out_specs=P("rep", None),
        check_vma=False,
    )
```

```python
import functools
import math

import jax
import jax.numpy as jnp
from jax import lax
from jax.experimental import pallas as pl
from jax.experimental.pallas import tpu as pltpu
from jax.sharding import PartitionSpec as P

D = 16384
INNER = 2
PARTS = 2
MESH = pl.DeviceIdType.MESH


def fused_kernel(
    outer,
    order,
    query_ref,
    key_ref,
    value_ref,
    lengths_ref,
    residual_ref,
    keys_hbm,
    values_hbm,
    weight_hbm,
    out_ref,
    keys,
    values,
    weight,
    context,
    x_out,
    x_in,
    z_out,
    z_in,
    totals,
    local_sem,
    weight_local,
    weight_send,
    weight_recv,
    context_sem,
    x_send,
    x_recv,
    z_send,
    z_recv,
    gz_send,
    gz_recv,
    gx_send,
    gx_recv,
    gs_send,
    gs_recv,
):
    tp = lax.axis_index("tp")
    sub = lax.axis_index("sub")
    z = lax.div(tp, INNER)
    x = lax.rem(tp, INNER)
    rows, head_dim = query_ref.shape
    all_rows, width = residual_ref.shape
    depth = weight_hbm.shape[0]
    slots = keys.shape[0] // rows

    other_core = {"sub": 1 - sub}
    other_x = {"tp": z * INNER + 1 - x}

    def along(k):
        return {"tp": lax.rem(z + k, outer) * INNER + x}

    def block_at(z_at, x_at, sub_at):
        first = ((z_at * INNER + x_at) * 2 + sub_at) * width
        return pl.ds(pl.multiple_of(first, width), width)

    barrier = pltpu.get_barrier_semaphore()
    partners = [other_core, other_x] + [along(k) for k in range(1, outer)]
    for partner in partners:
        pl.semaphore_signal(barrier, inc=1, device_id=partner, device_id_type=MESH)

    load_keys = pltpu.make_async_copy(keys_hbm, keys, local_sem.at[0])
    load_values = pltpu.make_async_copy(values_hbm, values, local_sem.at[1])
    load_keys.start()
    load_values.start()

    blocks = [(1 - x, k) for k in order] + [(x, k) for k in order]
    mine = pl.ds(pl.multiple_of(sub * depth, depth), depth)
    load_weight = []
    for j, (x_at, k) in enumerate(blocks):
        copy = pltpu.make_async_copy(
            weight_hbm.at[:, block_at(lax.rem(z + k, outer), x_at, sub)],
            weight.at[j, mine],
            weight_local.at[j],
        )
        copy.start()
        load_weight.append(copy)

    scale = 1.0 / math.sqrt(head_dim)
    query = query_ref[...]
    row = lax.broadcasted_iota(jnp.int32, (rows, 1), 0)
    filled = jnp.zeros((rows, 1), jnp.int32)
    for r in range(rows):
        filled = jnp.where(row == r, lengths_ref[r], filled)
    own = (
        jnp.sum(
            query.astype(jnp.float32) * key_ref[...].astype(jnp.float32), axis=1, keepdims=True
        )
        * scale
    )
    load_keys.wait()
    scores = (
        lax.dot_general(
            query, keys[...], (((1,), (1,)), ((), ())), preferred_element_type=jnp.float32
        )
        * scale
    )
    place = lax.broadcasted_iota(jnp.int32, scores.shape, 1) - row * slots
    valid = (place >= 0) & (place < filled)
    scores = jnp.where(valid, scores, -jnp.inf)
    top = jnp.maximum(jnp.max(scores, axis=1, keepdims=True), own)
    expo = jnp.exp(scores - top)
    expo_own = jnp.exp(own - top)
    total = jnp.sum(expo, axis=1, keepdims=True) + expo_own
    probs = (expo / total).astype(jnp.bfloat16)
    probs_own = (expo_own / total).astype(jnp.bfloat16)
    pl.semaphore_wait(barrier, len(partners))

    send_weight = []
    for j, (x_at, k) in enumerate(blocks):
        copy = pltpu.make_async_remote_copy(
            src_ref=weight_hbm.at[:, block_at(lax.rem(z + k, outer), x_at, 1 - sub)],
            dst_ref=weight.at[j, mine],
            send_sem=weight_send.at[j],
            recv_sem=weight_recv.at[j],
            device_id=other_core,
            device_id_type=MESH,
        )
        copy.start()
        send_weight.append(copy)

    load_values.wait()
    mixed = jnp.dot(probs, values[...], preferred_element_type=jnp.float32)
    mixed = mixed + probs_own.astype(jnp.float32) * value_ref[...].astype(jnp.float32)
    my_rows = pl.ds(pl.multiple_of(sub * rows, rows), rows)
    context[my_rows, :] = mixed.astype(jnp.bfloat16)
    send_context = pltpu.make_async_remote_copy(
        src_ref=context.at[my_rows],
        dst_ref=context.at[my_rows],
        send_sem=context_sem.at[0],
        recv_sem=context_sem.at[1],
        device_id=other_core,
        device_id_type=MESH,
    )
    send_context.start()
    send_context.wait_recv()
    whole_context = context[...]

    n = len(order)
    part = width // PARTS
    parts = [slice(p * part, (p + 1) * part) for p in range(PARTS)]
    sent = []

    def send(src, dst, device, send_sem, recv_sem):
        copy = pltpu.make_async_remote_copy(
            src_ref=src,
            dst_ref=dst,
            send_sem=send_sem,
            recv_sem=recv_sem,
            device_id=device,
            device_id_type=MESH,
        )
        copy.start()
        sent.append(copy)
        return copy

    x_copies = {}
    for p, cols in enumerate(parts):
        for j in range(n):
            if p == 0:
                load_weight[j].wait()
                send_weight[j].wait_recv()
            x_out[j, :, cols] = jnp.dot(
                whole_context, weight[j, :, cols], preferred_element_type=jnp.float32
            ).astype(jnp.bfloat16)
            x_copies[p, j] = send(
                x_out.at[j, :, cols],
                x_in.at[j, :, cols],
                other_x,
                x_send.at[p, j],
                x_recv.at[p, j],
            )
    for j in range(n):
        load_weight[n + j].wait()
        send_weight[n + j].wait_recv()
        totals[j] = jnp.dot(whole_context, weight[n + j], preferred_element_type=jnp.float32)
    z_copies = {}
    for p, cols in enumerate(parts):
        for j, k in enumerate(order):
            x_copies[p, j].wait_recv()
            both = totals[j, :, cols] + x_in[j, :, cols].astype(jnp.float32)
            if k == 0:
                totals[j, :, cols] = both
                continue
            z_out[k - 1, :, cols] = both.astype(jnp.bfloat16)
            z_copies[p, k] = send(
                z_out.at[k - 1, :, cols],
                z_in.at[k - 1, :, cols],
                along(k),
                z_send.at[p, k - 1],
                z_recv.at[p, k - 1],
            )

    hops = [0] + sorted([k for k in order if k > 0], key=lambda k: min(k, outer - k))

    def piece_at(k, x_at, sub_at, p):
        at = lax.rem(z + outer - k, outer)
        first = ((at * INNER + x_at) * 2 + sub_at) * width + p * part
        return out_ref.at[:, pl.ds(pl.multiple_of(first, part), part)]

    def whole_at(k, x_at):
        at = lax.rem(z + outer - k, outer)
        first = ((at * INNER + x_at) * 2 + sub) * width
        return out_ref.at[:, pl.ds(pl.multiple_of(first, width), width)]

    along_z = {}
    along_x = {}
    across = {}
    for p, cols in enumerate(parts):
        summed = totals[n - 1, :, cols] + residual_ref[:, cols].astype(jnp.float32)
        for k in order:
            if k > 0:
                z_copies[p, k].wait_recv()
                summed = summed + z_in[k - 1, :, cols].astype(jnp.float32)
        here = piece_at(0, x, sub, p)
        here[...] = summed.astype(jnp.bfloat16)
        along_x[p, 0] = send(here, here, other_x, gx_send.at[p, 0], gx_recv.at[p, 0])
        if p == PARTS - 1:
            block = whole_at(0, x)
            across[0] = send(block, block, other_core, gs_send.at[0], gs_recv.at[0])
        for k in hops[1:]:
            along_z[p, k] = send(
                here, here, along(k), gz_send.at[p, k - 1], gz_recv.at[p, k - 1]
            )
    def from_z(p, k):
        along_z[p, k].wait_recv()
        piece = piece_at(k, x, sub, p)
        along_x[p, k] = send(piece, piece, other_x, gx_send.at[p, k], gx_recv.at[p, k])
        if p == PARTS - 1:
            block = whole_at(k, x)
            across[k] = send(block, block, other_core, gs_send.at[k], gs_recv.at[k])

    def from_x(p, k):
        along_x[p, k].wait_recv()
        if p == PARTS - 1:
            block = whole_at(k, 1 - x)
            i = outer + k
            across[i] = send(block, block, other_core, gs_send.at[i], gs_recv.at[i])

    for p in range(PARTS + 1):
        for k in hops:
            if p < PARTS and k > 0:
                from_z(p, k)
            if p > 0:
                from_x(p - 1, k)
    for copy in across.values():
        copy.wait_recv()
    send_context.wait_send()
    for copy in send_weight + sent:
        copy.wait_send()


def per_device_fused(
    query, new_key, new_value, cache_keys, cache_values, lengths, out_weight, residual
):
    rows, _, head_dim = query.shape
    slots = cache_keys.shape[2]
    depth, columns = out_weight.shape
    all_rows, width = residual.shape
    outer = lax.axis_size("tp") // INNER
    order = [2, 1, 3, 0] if outer == 4 else [k for k in range(1, outer)] + [0]
    vmem = pl.BlockSpec(memory_space=pltpu.VMEM)
    anywhere = pl.BlockSpec(memory_space=pl.ANY)
    block = (all_rows, width)
    dma = pltpu.SemaphoreType.DMA
    return pl.pallas_call(
        functools.partial(fused_kernel, outer, order),
        out_shape=jax.ShapeDtypeStruct((all_rows, columns), jnp.bfloat16),
        in_specs=[vmem] * 3
        + [pl.BlockSpec(memory_space=pltpu.SMEM), vmem]
        + [anywhere] * 3,
        out_specs=vmem,
        scratch_shapes=[
            pltpu.VMEM((rows * slots, head_dim), jnp.bfloat16),
            pltpu.VMEM((rows * slots, head_dim), jnp.bfloat16),
            pltpu.VMEM((2 * outer, 2 * depth, width), jnp.bfloat16),
            pltpu.VMEM((all_rows, head_dim), jnp.bfloat16),
            pltpu.VMEM((outer, *block), jnp.bfloat16),
            pltpu.VMEM((outer, *block), jnp.bfloat16),
            pltpu.VMEM((outer - 1, *block), jnp.bfloat16),
            pltpu.VMEM((outer - 1, *block), jnp.bfloat16),
            pltpu.VMEM((outer, *block), jnp.float32),
            dma((2,)),
            dma((2 * outer,)),
            dma((2 * outer,)),
            dma((2 * outer,)),
            dma((2,)),
            dma((PARTS, outer)),
            dma((PARTS, outer)),
            dma((PARTS, outer - 1)),
            dma((PARTS, outer - 1)),
            dma((PARTS, outer - 1)),
            dma((PARTS, outer - 1)),
            dma((PARTS, outer)),
            dma((PARTS, outer)),
            dma((2 * outer,)),
            dma((2 * outer,)),
        ],
        compiler_params=pltpu.CompilerParams(
            collective_id=0, has_side_effects=True, vmem_limit_bytes=56 * 2**20
        ),
    )(
        query.reshape(rows, head_dim),
        new_key.reshape(rows, head_dim),
        new_value.reshape(rows, head_dim),
        lengths,
        residual,
        cache_keys.reshape(rows * slots, head_dim),
        cache_values.reshape(rows * slots, head_dim),
        out_weight,
    )


def per_device(query, new_key, new_value, cache_keys, cache_values, lengths, out_weight, residual):
    rows_here, heads_here, head_dim = query.shape
    slots = cache_keys.shape[2]
    scale = 1.0 / math.sqrt(head_dim)
    scores = (
        jnp.einsum("rhd,hrpd->hrp", query, cache_keys, preferred_element_type=jnp.float32) * scale
    )
    own = jnp.sum(query.astype(jnp.float32) * new_key.astype(jnp.float32), axis=-1) * scale
    own = jnp.transpose(own)
    valid = jnp.arange(slots)[None, None, :] < lengths[None, :, None]
    scores = jnp.where(valid, scores, -jnp.inf)
    top = jnp.maximum(jnp.max(scores, axis=-1), own)
    expo = jnp.exp(scores - top[:, :, None])
    expo_own = jnp.exp(own - top)
    total = jnp.sum(expo, axis=-1) + expo_own
    probs = (expo / total[:, :, None]).astype(jnp.bfloat16)
    probs_own = (expo_own / total).astype(jnp.bfloat16)
    mixed = jnp.einsum("hrp,hrpd->rhd", probs, cache_values, preferred_element_type=jnp.float32)
    mixed = mixed + jnp.transpose(probs_own).astype(jnp.float32)[:, :, None] * new_value.astype(
        jnp.float32
    )
    context = mixed.astype(jnp.bfloat16).reshape(rows_here, heads_here * head_dim)
    halves = lax.all_to_all(context, "sub", split_axis=1, concat_axis=0, tiled=True)
    all_rows = halves.shape[0]
    n_tp = lax.axis_size("tp")
    n_sub = lax.axis_size("sub")
    n_all = n_tp * n_sub
    width = D // n_all
    weight_view = out_weight.reshape(out_weight.shape[0], n_all, width)
    partial_value = jnp.einsum(
        "rk,kgc->grc", halves, weight_view, preferred_element_type=jnp.float32
    )
    arranged = partial_value.reshape(n_all, all_rows * width)
    summed = lax.psum_scatter(arranged, ("tp", "sub"), scatter_dimension=0, tiled=True)
    own_columns = summed.reshape(all_rows, width)
    updated = (residual.astype(jnp.float32) + own_columns).astype(jnp.bfloat16)
    gathered = lax.all_gather(
        updated.reshape(1, all_rows * width), ("tp", "sub"), axis=0, tiled=True
    )
    whole = jnp.transpose(gathered.reshape(n_all, all_rows, width), (1, 0, 2))
    return whole.reshape(all_rows, D)


def solution(mesh):
    n_tp, n_sub = mesh.shape["tp"], mesh.shape["sub"]
    width = D // (n_tp * n_sub)
    fused = n_sub == 2 and n_tp % INNER == 0 and 4 <= n_tp <= 16 and width % (128 * PARTS) == 0
    return jax.shard_map(
        per_device_fused if fused else per_device,
        mesh=mesh,
        in_specs=(
            P(("rep", "sub"), "tp", None),
            P(("rep", "sub"), "tp", None),
            P(("rep", "sub"), "tp", None),
            P("tp", ("rep", "sub"), None, None),
            P("tp", ("rep", "sub"), None, None),
            P(("rep", "sub")),
            P(("tp", "sub"), None),
            P("rep", ("tp", "sub")),
        ),
        out_specs=P("rep", None),
        check_vma=False,
    )
```
